32 devices in a mesh: seq: 8 (over z, x), dp: 4 (over y, core).
Axes of the slice: x: 2, y: 2, z: 4, core: 2. Of those that a mesh axis runs over, the one named last changes fastest.
Arguments:
- patches: bfloat16 [8, 4096, 4416], P('dp', 'seq'), may hold values from -6 to 6
- channel_mask: int32 [8, 69], P('dp'), may hold values 0 or 1
- lead_index: int32 [8], P('dp'), may hold values from 0 to 19
- patch_weight: float32 [4416, 768], P('seq'), may hold values from -0.09375 to 0.09375
- attention_weight: float32 [4, 768, 768], P(None, 'seq'), as said below
- forward_weight: float32 [2, 768, 3072], P(None, 'seq'), as said below
- vectors: float32 [25, 768], P(None, 'seq'), as said below
- patch_rows: float32 [4416], P('seq'), as said below
- patch_columns: float32 [768], replicated, as said below
- attention_rows: float32 [4, 768], P(None, 'seq'), as said below
- attention_columns: float32 [4, 768], replicated, as said below
- forward_rows: float32 [2, 768], P(None, 'seq'), as said below
- forward_columns: float32 [2, 3072], replicated, as said below
- vector_second: float32 [25, 768], P(None, 'seq'), as said below
- lead_average: float32 [20, 3], replicated, may hold values from 0.2 to 0.5
- output_cotangent: bfloat16 [8, 4096, 768], P('dp', 'seq'), may hold values from -6 to 6
- gate_cotangent: float32 [8, 3, 4096], P('dp', None, 'seq'), may hold values from -6 to 6
Outputs:
- block_output: bfloat16 [8, 4096, 768], P('dp', 'seq')
- expert_gates: float32 [8, 3, 4096], P('dp', None, 'seq')
- pixel_gradient: bfloat16 [8, 4096, 4416], P('dp', 'seq')
- patch_gradient: float32 [4416, 768], P('seq')
- attention_gradient: float32 [4, 768, 768], P(None, 'seq')
- forward_gradient: float32 [2, 768, 3072], P(None, 'seq')
- vector_gradient: float32 [25, 768], P(None, 'seq')
- patch_rows_new: float32 [4416], P('seq')
- patch_columns_new: float32 [768], replicated
- attention_rows_new: float32 [4, 768], P(None, 'seq')
- attention_columns_new: float32 [4, 768], replicated
- forward_rows_new: float32 [2, 768], P(None, 'seq')
- forward_columns_new: float32 [2, 3072], replicated
- vector_second_new: float32 [25, 768], P(None, 'seq')
- patch_weight_new: float32 [4416, 768], P('seq')
- attention_weight_new: float32 [4, 768, 768], P(None, 'seq')
- forward_weight_new: float32 [2, 768, 3072], P(None, 'seq')
- vectors_new: float32 [25, 768], P(None, 'seq')
- lead_stats: float32 [2, 20, 3], replicated
The draws below stay inside these ranges and needn't reach their ends.
Inputs may be any that keep to these rules, and one draw needn't show every extreme that they name: `attention_weight`: independent normal entries, a scale for each slice. `forward_weight`: independent normal entries, a scale for each slice. `vectors`: gains near 1; head rows and lead embeddings independent normal. `patch_rows`: Positive. `patch_columns`: Positive. `attention_rows`: Positive. `attention_columns`: Positive. `forward_rows`: Positive. `forward_columns`: Positive. `vector_second`: Positive.
All inputs are finite; a program needn't handle non-finite values. No bound on the sum of `channel_mask` on one device may be relied on, other than what follows from the above.
Results may differ from the reference program's by a relative error of at most 0.015.
Values may be sent and summed in bfloat16 or wider, within the bound.
No kernel may reach another device: no remote copies, remote signals or barrier semaphores. Data moves between devices by JAX's collectives and lax.ppermute only.
A program may use at most 448 MiB of HBM per device.

```python
import math
import jax
import jax.numpy as jnp
from jax import lax

D = 768
H = 12
HD = 64
FF = 3072
CH = 69
PIX = 64
LEADS = 20
FRAME = 4096
STEP = 10
P_SIZE = 4416
NV = 25
FRAMES = 8
TOKENS = 32768


def state_ratio():
    return STEP ** (-0.8) / (1.0 - STEP ** (-0.8))


def spread_factor(key, array_shape):
    return jnp.exp(jax.random.uniform(key, array_shape, jnp.float32, math.log(0.7), math.log(5.0)))


def falling_rows(key, array_shape, span):
    count = array_shape[-1]
    place = jnp.arange(count, dtype=jnp.float32) / max(count - 1, 1)
    jitter = jnp.exp(jax.random.uniform(key, array_shape, jnp.float32, math.log(0.8), math.log(1.25)))
    return 8.0 * jnp.exp(-math.log(span) * place) * jitter


def draw_attention_weight(key, part):
    key = jax.random.fold_in(key, 3)
    scales = jnp.array([(D / 2) ** (-0.5), (D / 2) ** (-0.5), D ** (-0.5), (D / 16) ** (-0.5)], jnp.float32)
    return jax.random.normal(key, (4, D, D), jnp.float32) * scales[:, None, None]


def draw_forward_weight(key, part):
    key = jax.random.fold_in(key, 5)
    scales = jnp.array([D ** (-0.5), FF ** (-0.5)], jnp.float32)
    return jax.random.normal(key, (2, D, FF), jnp.float32) * scales[:, None, None]


def draw_vectors(key, part):
    key = jax.random.fold_in(key, 7)
    first_key, second_key = jax.random.split(key)
    row_index = jnp.arange(NV)[:, None]
    gain_values = 1.0 + 0.3 * jax.random.uniform(first_key, (NV, D), jnp.float32, -1.0, 1.0)
    normal_values = jax.random.normal(second_key, (NV, D), jnp.float32)
    head_values = normal_values * (4 * D) ** (-0.5)
    lead_values = normal_values * 0.5
    return jnp.where(row_index < 2, gain_values, jnp.where(row_index < 5, head_values, lead_values))


def draw_patch_rows(key, part):
    key = jax.random.fold_in(key, 11)
    span = 12.0
    return state_ratio() * TOKENS * falling_rows(key, (P_SIZE,), span)


def draw_patch_columns(key, part):
    key = jax.random.fold_in(key, 13)
    return state_ratio() * TOKENS * 1.5 * spread_factor(key, (D,))


def draw_attention_rows(key, part):
    key = jax.random.fold_in(key, 17)
    span = 12.0
    scales = jnp.array([0.3, 0.3, 1.0, 0.05], jnp.float32) / 1.5
    return state_ratio() * TOKENS * scales[:, None] * falling_rows(key, (4, D), span)


def draw_attention_columns(key, part):
    key = jax.random.fold_in(key, 19)
    scales = jnp.array([0.3, 0.3, 1.0, 0.05], jnp.float32)
    return state_ratio() * TOKENS * scales[:, None] * spread_factor(key, (4, D))


def draw_forward_rows(key, part):
    key = jax.random.fold_in(key, 23)
    span = 12.0
    scales = jnp.array([0.13, 0.4], jnp.float32) / 1.5
    return state_ratio() * TOKENS * scales[:, None] * falling_rows(key, (2, D), span)


def draw_forward_columns(key, part):
    key = jax.random.fold_in(key, 29)
    scales = jnp.array([0.13, 0.4], jnp.float32)
    return state_ratio() * TOKENS * scales[:, None] * spread_factor(key, (2, FF))


def draw_vector_second(key, part):
    key = jax.random.fold_in(key, 31)
    row_index = jnp.arange(NV)[:, None]
    scales = jnp.where(row_index < 2, 0.5, jnp.where(row_index < 5, 0.3, 2.0 / LEADS))
    return state_ratio() * TOKENS * scales * spread_factor(key, (NV, D))


def touch_ends(drawn, stream_key, low, largest):
    spot = [jax.random.randint(jax.random.fold_in(stream_key, axis), (), 0, length) for axis, length in enumerate(drawn.shape)]
    longest = drawn.shape.index(max(drawn.shape))
    neighbour = spot[:longest] + [(spot[longest] + 1) % drawn.shape[longest]] + spot[longest + 1:]
    return drawn.at[tuple(spot)].set(low).at[tuple(neighbour)].set(largest)


def block_scale(key, shape, shards, least, largest):
    factor_of = 1.0
    for axis_at, blocks in shards:
        heights = jax.random.uniform(jax.random.fold_in(jax.random.fold_in(key, 6), axis_at), (blocks,), jnp.float32, least / len(shards), largest / len(shards))
        factor_of = factor_of * jnp.repeat(jnp.exp(heights), shape[axis_at] // blocks).reshape((-1,) + (1,) * (len(shape) - 1 - axis_at))
    return factor_of


def scatter_about(key, shape, scale, reach, cuts=(), kind=jnp.bfloat16):
    result = jax.random.normal(key, shape, jnp.float32) * scale
    if len(cuts) > 0:
        result = block_scale(key, shape, cuts, -0.22, 0.18) * result
    return jnp.clip(result, min=-reach, max=reach).astype(kind)


def setup_inputs(seed: int = 0) -> dict:
    keys = jax.random.split(jax.random.key(seed), 18)
    patches = scatter_about(keys[0], (FRAMES, FRAME, P_SIZE), 1.0, 6.0, ((0, 4), (1, 8)))
    channel_mask = touch_ends((jax.random.randint(keys[1], (FRAMES, CH), 0, 4) < 3).astype(jnp.int32), jax.random.fold_in(keys[1], 1), 0, 1)
    lead_index = touch_ends(jax.random.randint(keys[2], (FRAMES,), 0, LEADS), jax.random.fold_in(keys[2], 1), 0, LEADS - 1).astype(jnp.int32)
    patch_weight = scatter_about(keys[3], (P_SIZE, D), P_SIZE ** -0.5, 0.09375, ((0, 8),), jnp.float32)
    attention_weight = draw_attention_weight(jax.random.fold_in(keys[17], 71), 0)
    forward_weight = draw_forward_weight(jax.random.fold_in(keys[17], 71), 0)
    vectors = draw_vectors(jax.random.fold_in(keys[17], 71), 0)
    patch_rows = draw_patch_rows(jax.random.fold_in(keys[17], 71), 0)
    patch_columns = draw_patch_columns(jax.random.fold_in(keys[17], 71), 0)
    attention_rows = draw_attention_rows(jax.random.fold_in(keys[17], 71), 0)
    attention_columns = draw_attention_columns(jax.random.fold_in(keys[17], 71), 0)
    forward_rows = draw_forward_rows(jax.random.fold_in(keys[17], 71), 0)
    forward_columns = draw_forward_columns(jax.random.fold_in(keys[17], 71), 0)
    vector_second = draw_vector_second(jax.random.fold_in(keys[17], 71), 0)
    lead_average = jnp.clip(jax.random.uniform(keys[14], (LEADS, 3), jnp.float32, 0.2, 0.5), 0.2, 0.5)
    output_cotangent = scatter_about(keys[15], (FRAMES, FRAME, D), 1.0, 6.0, ((0, 4), (1, 8)))
    gate_cotangent = scatter_about(keys[16], (FRAMES, 3, FRAME), 1.0, 6.0, ((0, 4), (2, 8)), jnp.float32)
    return {"patches": patches, "channel_mask": channel_mask, "lead_index": lead_index, "patch_weight": patch_weight, "attention_weight": attention_weight, "forward_weight": forward_weight, "vectors": vectors, "patch_rows": patch_rows, "patch_columns": patch_columns, "attention_rows": attention_rows, "attention_columns": attention_columns, "forward_rows": forward_rows, "forward_columns": forward_columns, "vector_second": vector_second, "lead_average": lead_average, "output_cotangent": output_cotangent, "gate_cotangent": gate_cotangent}


@jax.custom_vjp
def low(v):
    return lax.optimization_barrier(v.astype(jnp.bfloat16)).astype(jnp.float32)

@jax.custom_vjp
def low_back(v):
    return v

def low_keep(v):
    return (low(v), None)

def low_pass(kept, grad):
    return (grad,)

def back_keep(v):
    return (v, None)

def back_low(kept, grad):
    return (low(grad),)
low.defvjp(low_keep, low_pass)
low_back.defvjp(back_keep, back_low)
norm_epsilon = 1e-06
square_floor = 1e-30
relative_rate = 1.0
clip_limit = 1.0
average_decay = 0.9
highest = lax.Precision.HIGHEST

def layer_norm(values, gain_row):
    center = lax.optimization_barrier(jnp.mean(values, -1, keepdims=True))
    shifted = values - center
    variance = lax.optimization_barrier(jnp.mean(shifted * shifted, -1, keepdims=True))
    return shifted * lax.rsqrt(variance + norm_epsilon) * gain_row

def attend(query_item, key_item, value_item):
    scores = low_back(jnp.einsum('qd,kd->qk', query_item, key_item, precision=highest) * HD ** (-0.5))
    weights = low(jax.nn.softmax(scores, axis=-1))
    return low(jnp.einsum('qk,kd->qd', weights, value_item, precision=highest))

def forward(patch_block, mask_block, lead_block, patch_f, attention_f, forward_f, vector_f):
    groups = patch_block.shape[0]
    tokens = groups * FRAME
    masked = (patch_block.reshape(groups, FRAME, CH, PIX) * mask_block[:, None, :, None]).reshape(tokens, P_SIZE)
    patch_low = low(patch_f)
    attention_low = low(attention_f)
    forward_low = low(forward_f)
    vector_low = low(vector_f)
    embedded = low_back(jnp.dot(masked, patch_low, precision=highest))
    lead_hot = (lead_block[:, None] == jnp.arange(LEADS, dtype=jnp.int32)[None, :]).astype(jnp.float32)
    lead_rows = jnp.dot(lead_hot, vector_low[5:], precision=highest)
    residual_zero = (embedded.reshape(groups, FRAME, D) + lead_rows[:, None, :]).reshape(tokens, D)
    normed_one = low(layer_norm(residual_zero, vector_low[0]))
    projected = [low_back(low(jnp.dot(normed_one, attention_low[number], precision=highest))) for number in range(3)]
    items = [value_part.reshape(groups, FRAME, H, HD).transpose(0, 2, 1, 3).reshape(groups * H, FRAME, HD) for value_part in projected]
    checked = jax.checkpoint(attend)
    attended = lax.map(lambda triple: checked(triple[0], triple[1], triple[2]), (items[0], items[1], items[2]))
    attended = low_back(attended.reshape(groups, H, FRAME, HD).transpose(0, 2, 1, 3).reshape(tokens, D))
    residual_one = residual_zero + low_back(jnp.dot(attended, attention_low[3], precision=highest))
    normed_two = low(layer_norm(residual_one, vector_low[1]))
    upward = low_back(jnp.dot(normed_two, forward_low[0], precision=highest))
    hidden = low(jax.nn.gelu(upward, approximate=False))
    residual_two = residual_one + low_back(jnp.dot(hidden, forward_low[1].T, precision=highest))
    logits = jnp.dot(residual_two, vector_low[2:5].T, precision=highest)
    expert_gates = jax.nn.softmax(logits, axis=-1)
    return (residual_two.reshape(groups, FRAME, D), expert_gates.reshape(groups, FRAME, 3).transpose(0, 2, 1))

def factored_step(gradient, rows_old, columns_old, master):
    decay_rate = 1.0 - STEP ** (-0.8)
    square = gradient * gradient + square_floor
    rows_new = decay_rate * rows_old + (1.0 - decay_rate) * lax.optimization_barrier(jnp.mean(square, 1))
    columns_new = decay_rate * columns_old + (1.0 - decay_rate) * lax.optimization_barrier(jnp.mean(square, 0))
    estimate = rows_new[:, None] * columns_new[None, :] / jnp.mean(rows_new)
    update = gradient * lax.rsqrt(estimate)
    ratio = jnp.sqrt(jnp.mean(update * update)) / clip_limit
    update = update / jnp.maximum(1.0, ratio)
    return (rows_new, columns_new, master - relative_rate * jnp.sqrt(jnp.mean(master * master)) * update)

def vector_step(gradient, second_old, master):
    decay_rate = 1.0 - STEP ** (-0.8)
    second_new = decay_rate * second_old + (1.0 - decay_rate) * (gradient * gradient + square_floor)
    update = gradient * lax.rsqrt(second_new)
    ratio = jnp.sqrt(lax.optimization_barrier(jnp.mean(update * update, 1, keepdims=True))) / clip_limit
    update = update / jnp.maximum(1.0, ratio)
    return (second_new, master - relative_rate * jnp.sqrt(lax.optimization_barrier(jnp.mean(master * master, 1, keepdims=True))) * update)

def reference(patches, channel_mask, lead_index, patch_weight, attention_weight, forward_weight, vectors, patch_rows, patch_columns, attention_rows, attention_columns, forward_rows, forward_columns, vector_second, lead_average, output_cotangent, gate_cotangent):
    patch_groups = patches.reshape(FRAMES, 1, FRAME, P_SIZE)
    mask_groups = channel_mask.astype(jnp.float32).reshape(FRAMES, 1, CH)
    lead_groups = lead_index.reshape(FRAMES, 1)
    output_groups = output_cotangent.reshape(FRAMES, 1, FRAME, D)
    gate_groups = gate_cotangent.reshape(FRAMES, 1, 3, FRAME)

    def group_step(totals, pieces):
        patch_block, mask_block, lead_block, output_block, gate_block = pieces

        def local_forward(patch_f, weight_e, weight_a, weight_m, weight_v):
            return forward(patch_f, mask_block, lead_block, weight_e, weight_a, weight_m, weight_v)
        outputs, pullback = jax.vjp(local_forward, patch_block.astype(jnp.float32), patch_weight, attention_weight, forward_weight, vectors)
        gradients = pullback((output_block.astype(jnp.float32), gate_block))
        totals = tuple((running + addend for running, addend in zip(totals, gradients[1:])))
        return (totals, (outputs[0].astype(jnp.bfloat16), outputs[1], gradients[0].astype(jnp.bfloat16)))
    initial = (jnp.zeros_like(patch_weight), jnp.zeros_like(attention_weight), jnp.zeros_like(forward_weight), jnp.zeros_like(vectors))
    totals, collected = lax.scan(group_step, initial, (patch_groups, mask_groups, lead_groups, output_groups, gate_groups))
    patch_gradient, attention_gradient, forward_gradient, vector_gradient = totals
    block_output = collected[0].reshape(FRAMES, FRAME, D)
    expert_gates = collected[1].reshape(FRAMES, 3, FRAME)
    pixel_gradient = collected[2].reshape(FRAMES, FRAME, P_SIZE)
    patch_rows_new, patch_columns_new, patch_weight_new = factored_step(patch_gradient, patch_rows, patch_columns, patch_weight)
    attention_rows_new, attention_columns_new, attention_weight_new = jax.vmap(factored_step)(attention_gradient, attention_rows, attention_columns, attention_weight)
    forward_rows_new, forward_columns_new, forward_weight_new = jax.vmap(factored_step)(forward_gradient, forward_rows, forward_columns, forward_weight)
    vector_second_new, vectors_new = vector_step(vector_gradient, vector_second, vectors)
    lead_hot = (lead_index[:, None] == jnp.arange(LEADS, dtype=jnp.int32)[None, :]).astype(jnp.float32)
    gate_frames = lax.optimization_barrier(jnp.sum(expert_gates, 2))
    lead_sums = jnp.dot(lead_hot.T, gate_frames, precision=highest)
    lead_counts = lax.optimization_barrier(jnp.sum(lead_hot, 0)) * FRAME
    batch_mean = jnp.where(lead_counts[:, None] > 0, lead_sums / jnp.maximum(lead_counts, 1.0)[:, None], lead_average)
    new_average = average_decay * lead_average + (1.0 - average_decay) * batch_mean
    lead_stats = jnp.stack([new_average, new_average / (1.0 - average_decay ** STEP)])
    return (block_output, expert_gates, pixel_gradient, patch_gradient, attention_gradient, forward_gradient, vector_gradient, patch_rows_new, patch_columns_new, attention_rows_new, attention_columns_new, forward_rows_new, forward_columns_new, vector_second_new, patch_weight_new, attention_weight_new, forward_weight_new, vectors_new, lead_stats)
```

```python
import functools
import math

import jax
import jax.numpy as jnp
from jax import lax
from jax.experimental.layout import Layout, with_layout_constraint
from jax.experimental import pallas as pl
from jax.experimental.pallas import tpu as pltpu
from jax.sharding import Mesh, PartitionSpec as P

H = 12
HD = 64
STEP = 10
SEQ = ("ring", "band")

norm_epsilon = 1e-06
square_floor = 1e-30
relative_rate = 1.0
clip_limit = 1.0
average_decay = 0.9
highest = lax.Precision.HIGHEST
log2_e = math.log2(math.e)
vmem_limit = 56 * 1024 * 1024
ONES = 16


def gelu_pair(values):
    cumulative = 0.5 + 0.5 * lax.erf(values * math.sqrt(0.5))
    density = jnp.exp(-0.5 * values * values) * (1.0 / math.sqrt(2.0 * math.pi))
    return values * cumulative, cumulative + values * density


def norm_forward(values, gain_row):
    center = jnp.mean(values, -1, keepdims=True)
    shifted = values - center
    variance = jnp.mean(shifted * shifted, -1, keepdims=True)
    inverse = lax.rsqrt(variance + norm_epsilon)
    standard = shifted * inverse
    return (standard * gain_row, standard, inverse)


def norm_backward(incoming, standard, inverse, gain_row):
    scaled_grad = incoming * gain_row
    first_mean = jnp.mean(scaled_grad, -1, keepdims=True)
    cross_mean = jnp.mean(scaled_grad * standard, -1, keepdims=True)
    return (
        inverse * (scaled_grad - first_mean - standard * cross_mean),
        jnp.sum(incoming * standard, (0, 1)),
    )


def dot(left, right):
    return jnp.dot(left, right, preferred_element_type=jnp.float32)


def dot_rows(left, right):
    return lax.dot_general(
        left, right, (((1,), (1,)), ((), ())), preferred_element_type=jnp.float32
    )


def forward_kernel(q_ref, k_ref, v_ref, o_ref, lse_ref, key_rows, value_ones):
    chunks, width = k_ref.shape[0], k_ref.shape[3]

    @pl.when(pl.program_id(1) == 0)
    def _():
        for c in range(chunks):
            key_rows[c] = jnp.transpose(jnp.concatenate([k_ref[c, 0], k_ref[c, 0]], 0))
            value_ones[c, :HD] = v_ref[c, 0]
            value_ones[c, HD:] = jnp.ones((ONES, width), jnp.bfloat16)

    scaled = q_ref[0, 0].astype(jnp.float32) * log2_e
    first = scaled.astype(jnp.bfloat16)
    rest = (scaled - first.astype(jnp.float32)).astype(jnp.bfloat16)
    query = jnp.concatenate([first, rest], 0)
    peak = None
    coming = dot(key_rows[0], query)
    for c in range(chunks):
        scores = coming
        if c + 1 < chunks:
            coming = dot(key_rows[c + 1], query)
        if c == 1:
            total = dot(value_ones[0], powered)
        elif c > 1:
            total = total * shrink + dot(value_ones[c - 1], powered)
        chunk_peak = jnp.max(scores, 0, keepdims=True)
        higher = chunk_peak if c == 0 else jnp.maximum(peak, chunk_peak)
        powered = jnp.exp2(scores - higher).astype(jnp.bfloat16)
        if c > 0:
            shrink = jnp.exp2(peak - higher)
        peak = higher
    last = dot(value_ones[chunks - 1], powered)
    total = last if chunks == 1 else total * shrink + last
    weight_sum = total[HD : HD + 1]
    o_ref[0, 0] = (total[:HD] / weight_sum).astype(jnp.bfloat16)
    lse_ref[0, 0] = (peak + jnp.log2(weight_sum)) * (1.0 / log2_e)


def append_row(block, row):
    first = row.astype(jnp.bfloat16).astype(jnp.float32)
    rest = row - first
    second = rest.astype(jnp.bfloat16).astype(jnp.float32)
    third = rest - second
    place = lax.broadcasted_iota(jnp.int32, block.shape, 0)
    extra = jnp.where(
        place == 0, first, jnp.where(place == 1, second, jnp.where(place == 2, third, 0.0))
    )
    return jnp.concatenate([block, extra.astype(jnp.bfloat16)], 0)


def backward_kernel(
    q_ref, g_ref, o_ref, lse_ref, k_ref, v_ref, *refs, merged
):
    dq_ref, dkv_ref = (refs[0], refs[0]) if merged else refs[:2]
    key_rows, value_rows, sums = refs[-3:]
    chunks, width = k_ref.shape[0], k_ref.shape[3]
    step = pl.program_id(1)

    @pl.when(step == 0)
    def _():
        ones = jnp.ones((HD, width), jnp.bfloat16)
        for c in range(chunks):
            key_rows[c] = jnp.transpose(jnp.concatenate([k_ref[c, 0], ones], 0))
            value_rows[c] = jnp.transpose(jnp.concatenate([v_ref[c, 0], ones], 0))
            sums[c] = jnp.zeros((2 * HD, width), jnp.float32)

    query = q_ref[0, 0]
    outgrad = g_ref[0, 0]
    row_dot = jnp.sum(
        outgrad.astype(jnp.float32) * o_ref[0, 0].astype(jnp.float32), 0, keepdims=True
    )
    query_columns = append_row(query, -lse_ref[0, 0])
    outgrad_columns = append_row(outgrad, -row_dot)
    def accumulate(c, query_grad, score_grad, weights):
        sums[c, :HD] += dot_rows(query, score_grad)
        sums[c, HD:] += dot_rows(outgrad, weights)
        part = dot(k_ref[c, 0], score_grad)
        return part if query_grad is None else query_grad + part

    query_grad = None
    coming = dot(key_rows[0], query_columns), dot(value_rows[0], outgrad_columns)
    for c in range(chunks):
        scores, prob_grad = coming
        if c + 1 < chunks:
            coming = dot(key_rows[c + 1], query_columns), dot(value_rows[c + 1], outgrad_columns)
        if c > 0:
            query_grad = accumulate(c - 1, query_grad, score_grad, weights)
        probs = jnp.exp2(scores * log2_e)
        score_grad = (probs * prob_grad).astype(jnp.bfloat16)
        weights = probs.astype(jnp.bfloat16)
    query_grad = accumulate(chunks - 1, query_grad, score_grad, weights)
    if merged:
        dq_ref[step, 0] = query_grad.astype(jnp.bfloat16)
    else:
        dq_ref[0, 0] = query_grad.astype(jnp.bfloat16)
    slot = 1 if merged else 0

    @pl.when(step == pl.num_programs(1) - 1)
    def _():
        for c in range(chunks):
            dkv_ref[c, slot] = sums[c, :HD].astype(dkv_ref.dtype)
            dkv_ref[c, slot + 1] = sums[c, HD:].astype(dkv_ref.dtype)


def run_forward(received, before, start=0, count=None):
    query = join_chunks(received)
    if before:
        query = tie(query, *before)
    if lax.axis_size("ring") == 1:
        triple = tuple((query, kind) for kind in range(3))
    else:
        frame = lax.all_gather(query[:, 1:], "ring", axis=0, tiled=True)
        triple = ((query, 0), (frame, 0), (frame, 1))
    count = query.shape[0] - start if count is None else count
    here, totals = attention_forward(*triple, start, count)
    return triple, here, totals


def token_block(slot, width, start=0):
    return pl.BlockSpec((1, 1, HD, width), lambda head, step: (step + start, slot, head, 0))


def frame_block(slot, chunks, width):
    return pl.BlockSpec((chunks, 1, HD, width), lambda head, step: (0, slot, head, 0))


def lse_block(width):
    return pl.BlockSpec((1, 1, 1, width), lambda head, step: (head, step, 0, 0))


def kernel_cost(matmuls, heads, queries, keys, moved):
    return pl.CostEstimate(
        flops=2 * matmuls * heads * queries * keys * HD * 4,
        bytes_accessed=moved,
        transcendentals=heads * queries * keys,
    )


def attention_forward(query, key, value, start, count):
    (q_array, q_slot), (k_array, k_slot), (v_array, v_slot) = query, key, value
    lanes, width = q_array.shape[2:]
    q_chunks = count
    k_chunks = k_array.shape[0]
    heads = lanes // HD
    return pl.pallas_call(
        forward_kernel,
        grid=(heads, q_chunks),
        in_specs=[
            token_block(q_slot, width, start),
            frame_block(k_slot, k_chunks, width),
            frame_block(v_slot, k_chunks, width),
        ],
        out_specs=[token_block(0, width), lse_block(width)],
        out_shape=[
            jax.ShapeDtypeStruct((q_chunks, 1, lanes, width), jnp.bfloat16),
            jax.ShapeDtypeStruct((heads, q_chunks, 1, width), jnp.float32),
        ],
        scratch_shapes=[
            pltpu.VMEM((k_chunks, width, 2 * HD), jnp.bfloat16),
            pltpu.VMEM((k_chunks, HD + ONES, width), jnp.bfloat16),
        ],
        compiler_params=pltpu.CompilerParams(
            dimension_semantics=("arbitrary", "arbitrary"), vmem_limit_bytes=vmem_limit
        ),
        cost_estimate=kernel_cost(
            2, heads, q_chunks * width, k_chunks * width, 8 * lanes * width * (q_chunks + k_chunks)
        ),
        name="attention_forward",
    )(q_array, k_array, v_array)


def attention_backward(query, outgrad, attended, lse, key, value, merged):
    (q_array, q_slot), (k_array, k_slot), (v_array, v_slot) = query, key, value
    g_array, g_slot = outgrad
    q_chunks, _, lanes, width = q_array.shape
    k_chunks = k_array.shape[0]
    heads = lanes // HD
    if merged:
        out_specs = [pl.BlockSpec((k_chunks, 3, HD, width), lambda head, step: (0, 0, head, 0))]
        out_shape = [jax.ShapeDtypeStruct((k_chunks, 3, lanes, width), jnp.bfloat16)]
    else:
        out_specs = [
            token_block(0, width),
            pl.BlockSpec((k_chunks, 2, HD, width), lambda head, step: (0, 0, head, 0)),
        ]
        out_shape = [
            jax.ShapeDtypeStruct((q_chunks, 1, lanes, width), jnp.bfloat16),
            jax.ShapeDtypeStruct((k_chunks, 2, lanes, width), jnp.float32),
        ]
    return pl.pallas_call(
        functools.partial(backward_kernel, merged=merged),
        grid=(heads, q_chunks),
        in_specs=[
            token_block(q_slot, width),
            token_block(g_slot, width),
            token_block(0, width),
            lse_block(width),
            frame_block(k_slot, k_chunks, width),
            frame_block(v_slot, k_chunks, width),
        ],
        out_specs=out_specs,
        out_shape=out_shape,
        scratch_shapes=[
            pltpu.VMEM((k_chunks, width, 2 * HD), jnp.bfloat16),
            pltpu.VMEM((k_chunks, width, 2 * HD), jnp.bfloat16),
            pltpu.VMEM((k_chunks, 2 * HD, width), jnp.float32),
        ],
        compiler_params=pltpu.CompilerParams(
            dimension_semantics=("arbitrary", "arbitrary"), vmem_limit_bytes=vmem_limit
        ),
        cost_estimate=kernel_cost(
            5, heads, q_chunks * width, k_chunks * width, 16 * lanes * width * (q_chunks + k_chunks)
        ),
        name="attention_backward",
    )(q_array, g_array, attended, lse, k_array, v_array)


def exchange(parts):
    if parts.shape[0] == 1:
        return parts
    return lax.all_to_all(parts, "band", 0, 0, tiled=True)


def join_chunks(parts):
    if lax.axis_size("ring") == 1:
        return parts
    bands, slots, lanes, width = parts.shape
    return jnp.transpose(parts, (1, 2, 0, 3)).reshape(1, slots, lanes, bands * width)


def split_chunks(parts, bands):
    if lax.axis_size("ring") == 1:
        return parts
    _, slots, lanes, width = parts.shape
    return jnp.transpose(parts.reshape(slots, lanes, bands, width // bands), (2, 0, 1, 3))


def other_core(value):
    return lax.ppermute(value, "core", [(0, 1), (1, 0)])


def core_half(value, axis, own):
    axis = axis % value.ndim
    half = value.shape[axis] // 2
    place = lax.axis_index("core") * half
    return lax.dynamic_slice_in_dim(value, place if own else half - place, half, axis)


def swap_pairs(value):
    return lax.ppermute(value, "pair", [(0, 1), (1, 0)])


def doubling():
    count = lax.axis_size("band")
    return (
        lax.axis_size("ring") == 1
        and count >= 4
        and count & (count - 1) == 0
        and lax.axis_size("pair") == 2
    )


def swap_bands(value, step):
    return lax.ppermute(value, "band", [(i, i ^ step) for i in range(lax.axis_size("band"))])


def both(value, received, bit, axis):
    first = bit == 0
    return jnp.stack(
        [jnp.where(first, value, received), jnp.where(first, received, value)], axis
    )


def pair_half(shard):
    rows = shard.shape[0] // 2
    return lax.dynamic_slice_in_dim(shard, lax.axis_index("pair") * rows, rows, 0)


def join_pairs(rows, count):
    value = rows.reshape(count, -1, rows.shape[1])
    return both(value, swap_pairs(value), lax.axis_index("pair"), 1).reshape(
        2 * rows.shape[0], rows.shape[1]
    )


def ring_gather(block, *gates, both_cores=False, marks=None, passed=None, beside=None):
    gates = [*gates, *[()] * lax.axis_size("band")]
    count = lax.axis_size("band")
    middle = count // 2
    order = [2 * z for z in range(middle)] + [2 * z + 1 for z in reversed(range(middle))]
    onward = [(order[p], order[(p + 1) % count]) for p in range(count)]
    back = [(target, source) for source, target in onward]
    band, core = lax.axis_index("band"), lax.axis_index("core")
    place = jnp.where(band % 2 == 0, band // 2, count - 1 - band // 2)
    half = block.shape[1]

    def put(blocks, part, at, column=0):
        at = (at + count) % count
        source = jnp.where(at < middle, 2 * at, 2 * (count - 1 - at) + 1)
        if both_cores:
            other = other_core(part)
            blocks = lax.dynamic_update_slice(
                blocks, other[None], (source, 0, column + (1 - core) * half)
            )
            column = column + core * half
        return lax.dynamic_update_slice(blocks, part[None], (source, 0, column))

    columns = 2 * half if both_cores else half
    blocks = put(jnp.zeros((count, block.shape[0], columns), block.dtype), block, place)
    first = second = block
    for step in range(1, middle):
        first, second = lax.optimization_barrier((first, second, *gates[step - 1]))[:2]
        if beside is not None and step > 1:
            passed.append(
                spread(tie(passed[-1] if passed else beside[None], first), count >> (step - 1))
            )
        first, second = lax.ppermute(first, "band", onward), lax.ppermute(second, "band", back)
        if marks is not None:
            marks.append((first, second))
        blocks = put(blocks, first, place - step)
        blocks = put(blocks, second, place + step)
    cut = -(-half // 256) * 128
    first, second = lax.optimization_barrier(
        (first[:, :cut], second[:, cut:], *gates[middle - 1], *(passed or ())[-2:-1])
    )[:2]
    while beside is not None and len(passed) < count.bit_length() - 1:
        passed.append(
            spread(tie(passed[-1] if passed else beside[None], first), count >> (len(passed) + 1))
        )
    first, second = lax.ppermute(first, "band", onward), lax.ppermute(second, "band", back)
    blocks = put(blocks, first, place - middle)
    return put(blocks, second, place - middle, cut)


def spread(value, step):
    bit = (lax.axis_index("band") // step) % 2
    value = both(value, swap_bands(value, step), bit, 1)
    return value.reshape(-1, *value.shape[2:])


def gather_doubling(shard, *gates):
    value, values = shard[None], []
    step = lax.axis_size("band") // 2
    gates = [*gates, *[()] * lax.axis_size("band")]
    while step:
        value = spread(tie(value, *gates[len(values)]), step)
        values.append(value)
        step //= 2
    return values


def halve(parts, step):
    parts = parts.reshape(-1, 2, *parts.shape[1:])
    bit = (lax.axis_index("band") // step) % 2
    sent = lax.dynamic_index_in_dim(parts, 1 - bit, 1, False)
    kept = lax.dynamic_index_in_dim(parts, bit, 1, False)
    total = kept.astype(jnp.float32) + swap_bands(sent, step).astype(jnp.float32)
    return total.astype(jnp.bfloat16)


def halve_pairs(parts):
    parts = parts.reshape(parts.shape[0], 2, -1, parts.shape[2])
    bit = lax.axis_index("pair")
    sent = lax.dynamic_index_in_dim(parts, 1 - bit, 1, False)
    kept = lax.dynamic_index_in_dim(parts, bit, 1, False)
    total = kept.astype(jnp.float32) + swap_pairs(sent).astype(jnp.float32)
    return total.astype(jnp.bfloat16)


def gather_bands(shard):
    return lax.all_gather(shard, SEQ, axis=0, tiled=True)


def in_order(own, other):
    first = lax.axis_index("core") == 0
    return jnp.concatenate([jnp.where(first, own, other), jnp.where(first, other, own)], -1)


def both_cores(own, other):
    return (own + other_core(other.astype(jnp.bfloat16)).astype(jnp.float32)).astype(jnp.bfloat16)


def sum_bands(total):
    if lax.axis_size("ring") > 1:
        return lax.psum_scatter(total, SEQ, scatter_dimension=0, tiled=True)
    bands = lax.axis_size("band")
    parts = total.reshape(bands, total.shape[0] // bands, total.shape[1])
    return jnp.sum(exchange(parts).astype(jnp.float32), 0).astype(jnp.bfloat16)


def sum_pairs(total):
    pairs = lax.axis_size("pair")
    if pairs == 1:
        return total
    if pairs == 2:
        return (total.astype(jnp.float32) + swap_pairs(total).astype(jnp.float32)).astype(total.dtype)
    return lax.psum(total, "pair")


def ordered(total):
    return in_order(total, other_core(total)).astype(jnp.float32)


def sum_everywhere(value):
    if not doubling():
        return lax.psum(value, SEQ)
    step = 1
    while step < lax.axis_size("band"):
        value = value + swap_bands(value, step)
        step *= 2
    return value


def tie(value, *others):
    return lax.optimization_barrier((value, *others))[0] if others else value


def as_line(scalars, width):
    line = jnp.concatenate([scalar.reshape(-1) for scalar in scalars])
    return jnp.pad(line, (0, width - line.size))[None]


def split_rows(rows, counts):
    results, place = [], 0
    for count in counts:
        results.append(rows[place : place + count])
        place += count
    return results


def factor_parts(gradient, rows_old, decay_rate):
    square = gradient * gradient + square_floor
    rows_new = decay_rate * rows_old + (1.0 - decay_rate) * jnp.mean(square, -1)
    ratio_part = jnp.sum(gradient * gradient / rows_new[..., None], -2)
    return rows_new, jnp.sum(square, -2), ratio_part, jnp.sum(rows_new, -1)


def lane(line, place):
    lanes = lax.broadcasted_iota(jnp.int32, line.shape, 1)
    return jnp.sum(jnp.where(lanes == place, line, 0.0), 1, keepdims=True)


def lanes_down(line, place, count):
    lanes = lax.broadcasted_iota(jnp.int32, (count, line.shape[1]), 1)
    rows = lax.broadcasted_iota(jnp.int32, (count, line.shape[1]), 0)
    return jnp.sum(jnp.where(lanes == rows + place, line, 0.0), 1, keepdims=True)


AT_ATTENTION, AT_FORWARD, AT_SQUARES, AT_VECTOR_SQUARES, AT_VECTOR_SIZES = 0, 4, 6, 128, 256
ROW_ATTENTION, ROW_FORWARD, ROW_LINE, ROW_SMALL = 0, 8, 24, 25


def patch_kernel(core_ref, own_ref, other_ref, rows_ref, grad_ref, rows_new_ref, pack_ref):
    decay_rate = 1.0 - STEP ** (-0.8)
    own, other = own_ref[...].astype(jnp.float32), other_ref[...].astype(jnp.float32)
    first = core_ref[0] == 0
    gradient = jnp.concatenate(
        [jnp.where(first, own, other), jnp.where(first, other, own)], 1
    )
    grad_ref[...] = gradient
    plain = gradient * gradient
    square = plain + square_floor
    rows_new = decay_rate * rows_ref[...] + (1.0 - decay_rate) * jnp.mean(square, 1, keepdims=True)
    rows_new_ref[...] = rows_new
    width = gradient.shape[1]
    pack = jnp.concatenate(
        [
            jnp.sum(square, 0, keepdims=True),
            jnp.sum(plain / rows_new, 0, keepdims=True),
            jnp.broadcast_to(jnp.sum(rows_new, 0, keepdims=True), (1, width)),
            jnp.zeros((5, width), jnp.float32),
        ],
        0,
    )
    for copy in range(pack_ref.shape[0]):
        pack_ref[copy] = pack


def patch_statistics(own, other, rows_old, copies):
    rows, half = own.shape
    width = 2 * half
    space = [pl.BlockSpec(memory_space=pltpu.VMEM)]
    return pl.pallas_call(
        patch_kernel,
        in_specs=[pl.BlockSpec(memory_space=pltpu.SMEM)] + space * 3,
        out_specs=space * 3,
        out_shape=[
            jax.ShapeDtypeStruct((rows, width), jnp.float32),
            jax.ShapeDtypeStruct((rows, 1), jnp.float32),
            jax.ShapeDtypeStruct((copies, 8, width), jnp.float32),
        ],
        compiler_params=pltpu.CompilerParams(vmem_limit_bytes=vmem_limit),
        name="patch_statistics",
    )(lax.axis_index("core").reshape(1), own, other, rows_old.reshape(rows, 1))


def finish_matrix(
    grad, master, rows_new, olds, sums, ratios, rows_total, weight_total, band_count, store
):
    decay_rate = 1.0 - STEP ** (-0.8)
    width = sums[0].shape[1]
    row_count = grad.shape[0] * band_count
    element_count = row_count * width * len(olds)
    columns_new = [
        decay_rate * old + (1.0 - decay_rate) / row_count * part for old, part in zip(olds, sums)
    ]
    mean_rows = rows_total / row_count
    spread_sum = sum(
        jnp.sum(ratio / column, 1, keepdims=True) for ratio, column in zip(ratios, columns_new)
    )
    mean_square = mean_rows * spread_sum / element_count
    shrink = jnp.maximum(1.0, jnp.sqrt(mean_square) / clip_limit)
    rate_value = relative_rate * jnp.sqrt(weight_total / element_count)
    row_scale = lax.rsqrt(rows_new) * (jnp.sqrt(mean_rows) * rate_value / shrink)
    for piece, column in enumerate(columns_new):
        part = slice(piece * width, (piece + 1) * width)
        store(part, column, master[:, part] - grad[:, part] * row_scale * lax.rsqrt(column))


def patch_finish_kernel(
    pack_ref, square_ref, grad, master, rows_new, columns, master_new, columns_new, *, band_count
):
    pack = jnp.sum(pack_ref[...], 0)

    def store(part, column, value):
        master_new[:, part] = value
        columns_new[:, part] = column

    finish_matrix(
        grad,
        master,
        rows_new[...],
        [columns[...]],
        [pack[0:1]],
        [pack[1:2]],
        pack[2:3, :1],
        square_ref[...],
        band_count,
        store,
    )


def rest_finish_kernel(
    pack_ref,
    attention_grad, attention_master, attention_rows, attention_columns,
    forward_grad, forward_master, forward_rows, forward_columns,
    vectors, vector_update, lead_average,
    attention_new, attention_columns_new, forward_new, forward_columns_new,
    vectors_new, lead_new, patch_square,
    *, band_count,
):
    pack = jnp.sum(pack_ref[...], 0)
    width = pack.shape[1]
    line = pack[ROW_LINE : ROW_LINE + 1, :512]
    patch_square[...] = lane(line, AT_SQUARES + 6)
    for k in range(4):
        def attention_store(part, column, value):
            attention_new[k, :, part] = value
            attention_columns_new[k : k + 1, part] = column

        row = ROW_ATTENTION + k
        finish_matrix(
            attention_grad.at[k],
            attention_master.at[k],
            attention_rows[k],
            [attention_columns[k : k + 1, :]],
            [pack[row : row + 1]],
            [pack[row + 4 : row + 5]],
            lane(line, AT_ATTENTION + k),
            lane(line, AT_SQUARES + 2 + k),
            band_count,
            attention_store,
        )
    pieces = forward_grad.shape[2] // width
    for k in range(2):
        def forward_store(part, column, value):
            forward_new[k, :, part] = value
            forward_columns_new[k : k + 1, part] = column

        rows = [ROW_FORWARD + 2 * piece + k for piece in range(pieces)]
        finish_matrix(
            forward_grad.at[k],
            forward_master.at[k],
            forward_rows[k],
            [forward_columns[k : k + 1, p * width : (p + 1) * width] for p in range(pieces)],
            [pack[row : row + 1] for row in rows],
            [pack[row + 2 * pieces : row + 2 * pieces + 1] for row in rows],
            lane(line, AT_FORWARD + k),
            lane(line, AT_SQUARES + k),
            band_count,
            forward_store,
        )
    count = vectors.shape[0]
    vector_squares = lanes_down(line, AT_VECTOR_SQUARES, count)
    vector_sizes = lanes_down(line, AT_VECTOR_SIZES, count)
    vector_shrink = jnp.maximum(1.0, jnp.sqrt(vector_squares / width) / clip_limit)
    vector_rate = relative_rate * jnp.sqrt(vector_sizes / width)
    vectors_new[...] = vectors[...] - vector_rate / vector_shrink * vector_update[...]
    sums = pack[ROW_SMALL : ROW_SMALL + 1, :128]
    counts = pack[ROW_SMALL : ROW_SMALL + 1, 128:256]
    average = lead_average[...]
    batch_mean = jnp.where(counts > 0, sums / jnp.maximum(counts, 1.0), average)
    new_average = average_decay * average + (1.0 - average_decay) * batch_mean
    lead_new[0:1] = new_average
    lead_new[1:2] = new_average / (1.0 - average_decay**STEP)


def in_vmem(kernel, name, arguments, shapes, **fixed):
    space = pl.BlockSpec(memory_space=pltpu.VMEM)
    return pl.pallas_call(
        functools.partial(kernel, **fixed),
        in_specs=[space] * len(arguments),
        out_specs=[space] * len(shapes),
        out_shape=[jax.ShapeDtypeStruct(shape, jnp.float32) for shape in shapes],
        compiler_params=pltpu.CompilerParams(vmem_limit_bytes=vmem_limit),
        name=name,
    )(*arguments)


def finish_patch(pack, square, gradient, master, rows_new, columns, band_count):
    columns = columns.reshape(1, -1)
    arguments = (pack, square, gradient, master, rows_new, columns)
    return in_vmem(
        patch_finish_kernel,
        "patch_finish",
        arguments,
        (master.shape, columns.shape),
        band_count=band_count,
    )


def finish_rest(pack, attention, forward, vectors, vector_update, lead_average, band_count):
    def columns(parts):
        return (parts[0], parts[1], parts[2].reshape(*parts[2].shape, 1), parts[3])

    lead_line = jnp.pad(lead_average.reshape(1, -1), ((0, 0), (0, 128 - lead_average.size)))
    arguments = (pack, *columns(attention), *columns(forward), vectors, vector_update, lead_line)
    shapes = [array.shape for parts in (attention, forward) for array in (parts[1], parts[3])]
    shapes += [vectors.shape, (2, 128), (1, 1)]
    return in_vmem(rest_finish_kernel, "rest_finish", arguments, shapes, band_count=band_count)


def local(
    patches,
    channel_mask,
    lead_index,
    patch_weight,
    attention_weight,
    forward_weight,
    vectors,
    patch_rows,
    patch_columns,
    attention_rows,
    attention_columns,
    forward_rows,
    forward_columns,
    vector_second,
    lead_average,
    output_cotangent,
    gate_cotangent,
):
    low = jnp.bfloat16
    frames, frame_rows, patch_width = patches.shape
    channels = channel_mask.shape[1]
    bands, rings = lax.axis_size("band"), lax.axis_size("ring")
    band_count = bands * rings
    width = patch_weight.shape[1]
    half = width // 2
    lead_count = vectors.shape[0] - 5
    share = attention_weight.shape[1]
    vector_columns = vectors.shape[1]
    heads = frames * H // bands
    groups = H // heads
    decay_rate = 1.0 - STEP ** (-0.8)
    pair = lax.axis_index("pair")

    def weight_square(master):
        return jnp.sum(master * master, (-2, -1))

    squares = jnp.concatenate(
        [
            weight_square(forward_weight),
            weight_square(attention_weight),
            weight_square(patch_weight).reshape(1),
            jnp.sum(vectors * vectors, -1),
        ]
    )
    kinds = attention_weight[:3] * jnp.array([HD ** (-0.5), 1.0, 1.0], jnp.float32)[:, None, None]
    kinds = kinds.astype(low).reshape(3, share, groups, heads, HD)
    kinds = [
        jnp.transpose(kinds[:, :, :, j], (1, 2, 0, 3)).reshape(share, width) for j in range(heads)
    ]
    vector_part = jnp.pad(vectors.T.astype(low), ((0, 0), (0, 256 - vectors.shape[0])))
    first_shard = jnp.concatenate(
        [core_half(piece, 1, True) for piece in (kinds[0], vector_part)], 1
    )
    later_shard = jnp.concatenate(
        [core_half(piece, 1, True) for piece in (*kinds[1:], attention_weight[3].astype(low))], 1
    )
    patch_own = core_half(patch_weight, 1, True).astype(low)
    if doubling():
        marks, passed = [], []
        patch_full = ring_gather(
            patch_own, [], [first_shard], both_cores=True, marks=marks, passed=passed,
            beside=first_shard,
        )
        patch_full = patch_full.reshape(patch_width, width)
        first_own = passed[-1].reshape(width, first_shard.shape[1])
        later_steps = gather_doubling(pair_half(later_shard), [patch_full])
    else:
        first_own = gather_bands(first_shard)
        patch_own = gather_bands(patch_own)
        patch_full = in_order(patch_own, other_core(patch_own))
        later_steps = []
    first_other = other_core(first_own)
    projections = [in_order(first_own[:, :half], first_other[:, :half])]
    vector_full = in_order(first_own[:, half:], first_other[:, half:])[:, : vectors.shape[0]].T
    vector_full = vector_full.astype(jnp.float32)
    patch_full, squares = lax.optimization_barrier((patch_full, squares))
    hidden_half = forward_weight.shape[2] // 2
    forward_shard = core_half(forward_weight, 2, True).astype(low)
    forward_shard = jnp.concatenate([forward_shard[0], forward_shard[1]], 1)
    mask_values = channel_mask.astype(low)
    masked = (
        patches.reshape(frames, frame_rows, channels, patch_width // channels)
        * mask_values[:, None, :, None]
    ).reshape(frames, frame_rows, patch_width)
    embedded = jnp.einsum("fsp,pd->fsd", masked, patch_full, preferred_element_type=jnp.float32)
    lead_hot = (lead_index[:, None] == jnp.arange(lead_count, dtype=jnp.int32)[None, :]).astype(
        jnp.float32
    )
    lead_rows = jnp.dot(lead_hot, vector_full[5:], precision=highest)
    residual_zero = embedded + lead_rows[:, None, :]
    gain_one, gain_two, head_rows = vector_full[0], vector_full[1], vector_full[2:5]
    normed_one, standard_one, inverse_one = norm_forward(residual_zero, gain_one)
    normed_one = normed_one.astype(low)

    if doubling():
        normed_one = tie(normed_one, later_steps[-2])
    def project(j, *before):
        projected = jnp.einsum(
            "dm,fsd->fms", projections[j], tie(normed_one, *before), preferred_element_type=jnp.float32
        ).astype(low)
        return projected.reshape(bands, 3, HD, frame_rows)

    received, triples, attended_here, log_totals = [], [], [], []

    def run_head(number, before):
        triple, here, totals = run_forward(received[number], before)
        triples.append(triple)
        attended_here.append(here)
        log_totals.append(totals)

    first_sent = project(0)
    received.append(exchange(first_sent))
    if doubling():
        later_own = tie(later_steps[-1], first_sent).reshape(-1, later_shard.shape[1])
        later_own = join_pairs(later_own, bands)
    else:
        later_own = gather_bands(later_shard)
    later_other = other_core(later_own)
    projections += [
        in_order(later_own[:, j * half : (j + 1) * half], later_other[:, j * half : (j + 1) * half])
        for j in range(heads - 1)
    ]
    place = (heads - 1) * half
    output_weight = in_order(later_own[:, place:], later_other[:, place:])
    second_sent = [project(1)] if heads > 1 else []
    marks = []
    if doubling():
        forward_own = ring_gather(pair_half(forward_shard), second_sent, marks=marks)
        forward_own = forward_own.reshape(-1, 2 * hidden_half)
    else:
        forward_own = gather_bands(forward_shard)
    forward_parts = forward_own[:, :hidden_half], forward_own[:, hidden_half:]
    swapped = ()
    if doubling():
        forward_parts = tuple(part.reshape(bands, -1, hidden_half) for part in forward_parts)
        swapped = tuple(swap_pairs(part) for part in forward_parts)

    def forward_half(number):
        part = forward_parts[number]
        if doubling():
            part, received, _ = lax.optimization_barrier(
                (part, swapped[number], attended_here[-1])
            )
            part = both(part, received, pair, 1).reshape(width, hidden_half)
        return part, other_core(part)

    for j in range(1, heads):
        sent = second_sent[0] if j == 1 else project(j)
        sent = tie(sent, received[j - 1], *attended_here[j - 2 : j - 1])
        received.append(exchange(sent))
        before = [sent] if j == 1 else [attended_here[-1]]
        before += [part for step in marks[1:2] for part in step if j == 2]
        run_head(j - 1, before)
    before = [forward_own, *attended_here[-1:]]
    chunks = received[-1].shape[0]
    if rings == 1 and heads > 1 and chunks % 4 == 0:
        triple, here, totals = run_forward(received[-1], before, 0, chunks * 3 // 4)
        attended = exchange(tie(jnp.concatenate(attended_here, 1), received[-1]))
        _, here_end, totals_end = run_forward(
            received[-1], [here, attended, *swapped[:1]], chunks * 3 // 4, chunks // 4
        )
        triples.append(triple)
        attended_here.append(jnp.concatenate([here, here_end], 0))
        log_totals.append(jnp.concatenate([totals, totals_end], 1))
        attended = jnp.concatenate([attended, exchange(attended_here[-1])], 1)
    else:
        run_head(heads - 1, before)
        attended = jnp.concatenate([split_chunks(here, bands) for here in attended_here], 1)
        attended = exchange(attended)
    attended = attended.reshape(frames, width, frame_rows)
    up_halves, down_halves = forward_half(0), forward_half(1)

    residual_one = residual_zero + jnp.einsum(
        "fns,nd->fsd", attended, output_weight, preferred_element_type=jnp.float32
    )
    normed_two, standard_two, inverse_two = norm_forward(residual_one, gain_two)
    normed_two = normed_two.astype(low)

    hidden, slopes = [], []
    residual_two = residual_one
    for up, down in zip(up_halves, down_halves):
        upward = jnp.einsum("fsd,dh->fsh", normed_two, up, preferred_element_type=jnp.float32)
        activated, slope = gelu_pair(upward)
        hidden.append(activated.astype(low))
        slopes.append(slope)
        residual_two = residual_two + jnp.einsum(
            "fsh,dh->fsd", hidden[-1], down, preferred_element_type=jnp.float32
        )
    logits = jnp.einsum("fsd,ed->fes", residual_two, head_rows, precision=highest)
    expert_gates = jax.nn.softmax(logits, axis=1)
    logit_grad = expert_gates * (
        gate_cotangent - jnp.sum(expert_gates * gate_cotangent, 1, keepdims=True)
    )
    adjoint_two = output_cotangent.astype(jnp.float32) + jnp.einsum(
        "fes,ed->fsd", logit_grad, head_rows, precision=highest
    )
    adjoint_two_low = adjoint_two.astype(low)
    upward_grad = []
    normed_two_grad = 0.0
    for up, down, slope in zip(up_halves, down_halves, slopes):
        hidden_grad = jnp.einsum(
            "fsd,dh->fsh", adjoint_two_low, down, preferred_element_type=jnp.float32
        )
        upward_grad.append((hidden_grad * slope).astype(low))
        normed_two_grad = normed_two_grad + jnp.einsum(
            "fsh,dh->fsd", upward_grad[-1], up, preferred_element_type=jnp.float32
        )
    through_two, gain_two_grad = norm_backward(normed_two_grad, standard_two, inverse_two, gain_two)
    adjoint_one = adjoint_two + through_two
    adjoint_one_low = adjoint_one.astype(low)
    attended_grad = jnp.einsum(
        "fsd,nd->fns", adjoint_one_low, output_weight, preferred_element_type=jnp.float32
    ).astype(low)
    attended_grad = attended_grad.reshape(bands, 1, heads, HD, frame_rows)
    first_outgrad = attended_grad[:, :, 0]
    first_grad = exchange(first_outgrad)
    outgrads = [(join_chunks(first_grad), 0)]
    if heads > 1:
        later_sent = attended_grad[:, 0, 1:]

    early_left = lax.optimization_barrier((normed_two, adjoint_two_low, first_outgrad))[:2]

    def early_product(left, right):
        return jnp.einsum("fsd,fsh->dh", left, right, preferred_element_type=jnp.float32)

    early = jnp.concatenate(
        [
            both_cores(early_product(left, right[0]), early_product(left, right[1]))
            for left, right in zip(early_left, (upward_grad, hidden))
        ],
        1,
    )
    outgrads[0] = (tie(outgrads[0][0], early), 0)
    if heads > 1:
        later = join_chunks(exchange(tie(later_sent, first_grad, early)))
        outgrads += [(later, j) for j in range(heads - 1)]
    early_stages = []
    if doubling():
        stage = halve_pairs(early.reshape(bands, -1, early.shape[1]))
        early_stages.append(stage)
        step = 1
        while step < bands and len(early_stages) < heads:
            if step == 1:
                stage = tie(stage, first_grad)
            stage = halve(stage, step)
            early_stages.append(stage)
            step *= 2

    head_grads = []
    for j in range(heads):
        query, key, value = triples[j]
        outgrad = outgrads[j]
        if j > 0:
            outgrad = (
                tie(outgrad[0], grads, *early_stages[j - 1 : j], *head_grads[j - 2 : j - 1]),
                outgrad[1],
            )
        grads = attention_backward(
            query, outgrad, attended_here[j], log_totals[j], key, value, rings == 1
        )
        if rings == 1:
            parts = grads[0]
        else:
            parts = lax.psum_scatter(grads[1], "ring", scatter_dimension=0, tiled=True)
            parts = jnp.concatenate([grads[0], parts.astype(low)], 1)
        parts = exchange(tie(split_chunks(parts, bands), *head_grads[j - 1 : j]))
        head_grads.append(parts.reshape(frames, width, frame_rows))
    kernel_end = (*grads, *early_stages[heads - 1 : heads], *head_grads[heads - 2 : heads - 1])
    head_grads = [tie(part, *kernel_end) for part in head_grads[:-1]] + head_grads[-1:]

    normed_one_grad = 0.0
    for j in range(heads):
        normed_one_grad = normed_one_grad + jnp.einsum(
            "fms,dm->fsd", head_grads[j], projections[j], preferred_element_type=jnp.float32
        )
    through_one, gain_one_grad = norm_backward(normed_one_grad, standard_one, inverse_one, gain_one)
    adjoint_zero = adjoint_one + through_one
    adjoint_zero_low = adjoint_zero.astype(low)

    def projection_product(j, own_half):
        if j == heads:
            return jnp.einsum(
                "fns,fsd->nd",
                attended,
                core_half(tie(adjoint_one_low, *kernel_end), 2, own_half),
                preferred_element_type=jnp.float32,
            )
        return jnp.einsum(
            "fsd,fms->dm",
            normed_one,
            core_half(head_grads[j], 1, own_half),
            preferred_element_type=jnp.float32,
        )

    def projection_part(numbers):
        return both_cores(
            jnp.concatenate([projection_product(j, True) for j in numbers], 1),
            jnp.concatenate([projection_product(j, False) for j in numbers], 1),
        )

    def projection_start(total):
        if doubling():
            return halve_pairs(total.reshape(bands, -1, total.shape[1]))
        return total

    def projection_exchange(total):
        return exchange(total) if doubling() else sum_bands(total)

    def projection_sums(total):
        if doubling():
            return join_pairs(jnp.sum(total.astype(jnp.float32), 0).astype(low), 1)
        return sum_pairs(total)

    earlier = projection_part([*range(heads - 1), heads])

    def patch_product(columns):
        return jnp.einsum("fsp,fsd->pd", masked, columns, preferred_element_type=jnp.float32)

    own_adjoint = core_half(adjoint_zero_low, 2, True)
    other_adjoint = core_half(adjoint_zero_low, 2, False)
    cut = half * 2 // 3
    pieces = [
        both_cores(
            patch_product(own_adjoint[:, :, piece]), patch_product(other_adjoint[:, :, piece])
        )
        for piece in (slice(0, cut), slice(cut, half))
    ]
    sent = tuple(pieces)
    first_piece = sum_bands(pieces[0])

    pixel_term = jnp.einsum(
        "fsd,pd->fsp", tie(adjoint_zero_low, *sent), patch_full, preferred_element_type=jnp.float32
    )
    pixel_gradient = (
        (
            pixel_term.reshape(frames, frame_rows, channels, -1)
            * mask_values.astype(jnp.float32)[:, None, :, None]
        )
        .reshape(frames, frame_rows, patch_width)
        .astype(low)
    )

    head_grads[-1] = tie(head_grads[-1], *sent)
    lead_sums = jnp.dot(lead_hot.T, jnp.sum(tie(expert_gates, *sent), 2), precision=highest)
    lead_counts = jnp.sum(lead_hot, 0) * frame_rows
    small = jnp.concatenate(
        [
            jnp.pad(value, (0, 128 - value.size))
            for value in (lead_sums.reshape(-1), jnp.repeat(lead_counts, 3))
        ]
    )
    small = jnp.pad(small, (0, width - small.size))[None]
    if lax.axis_size("pair") == 2:
        small = small + swap_pairs(small)
    elif lax.axis_size("pair") > 1:
        small = lax.psum(small, "pair")
    small = small + other_core(small)
    lead_term = jnp.dot(lead_hot.T, jnp.sum(tie(adjoint_zero, *sent), 1), precision=highest)
    head_gradient = jnp.einsum(
        "fes,fsd->ed", tie(logit_grad, *sent), residual_two, precision=highest
    )
    vector_term = jnp.concatenate(
        [gain_one_grad[None], gain_two_grad[None], head_gradient, lead_term], 0
    )
    vector_term = jnp.pad(vector_term.T, ((0, 0), (0, 128 - vectors.shape[0])))
    total = jnp.concatenate(
        [earlier, projection_part([heads - 1]), both_cores(vector_term, vector_term)], 1
    )
    total = projection_start(total)
    total = projection_exchange(tie(total, first_piece, pixel_gradient))
    second_piece = sum_bands(tie(pieces[1], total))
    total = projection_sums(total)
    place = (heads + 1) * half
    vector_gradient = total[:, place : place + vectors.shape[0]].T.astype(jnp.float32)
    total = total[:, :place]
    total_other = other_core(total)
    parts = [
        in_order(total[:, j * half : (j + 1) * half], total_other[:, j * half : (j + 1) * half])
        for j in range(heads + 1)
    ]
    output_gradient = parts.pop(heads - 1)
    projection_gradient = jnp.transpose(
        jnp.stack(parts).reshape(heads, share, groups, 3, HD), (3, 1, 2, 0, 4)
    ).reshape(3, share, width)
    kind_scales = jnp.array([HD ** (-0.5), 1.0, 1.0, 1.0], jnp.float32)[:, None, None]
    attention_gradient = with_layout_constraint(
        jnp.concatenate([projection_gradient, output_gradient[None]], 0).astype(jnp.float32)
        * kind_scales,
        Layout(major_to_minor=(0, 1, 2)),
    )

    if doubling():
        stage = tie(early_stages[-1], *sent)
        step = 1 << (len(early_stages) - 1)
        while step < bands:
            stage = halve(stage, step)
            step *= 2
        early = join_pairs(stage[0], 1)
    else:
        early = sum_pairs(sum_bands(tie(early, *sent)))
    early_other = other_core(early)
    forward_gradient = jnp.stack(
        [
            in_order(early[:, :hidden_half], early_other[:, :hidden_half]),
            in_order(early[:, hidden_half:], early_other[:, hidden_half:]),
        ]
    ).astype(jnp.float32)
    units = forward_weight.shape[2]
    forward_rows_new, forward_sums, forward_ratios, forward_total = factor_parts(
        forward_gradient, forward_rows, decay_rate
    )

    vector_second_new = decay_rate * vector_second + (1.0 - decay_rate) * (
        vector_gradient * vector_gradient + square_floor
    )
    vector_update = vector_gradient * lax.rsqrt(vector_second_new)
    vector_squares = jnp.sum(vector_update * vector_update, -1)

    attention_rows_new, attention_sums, attention_ratios, attention_total = factor_parts(
        attention_gradient, attention_rows, decay_rate
    )
    pieces = units // width
    line = jnp.concatenate(
        [
            jnp.pad(value, (0, 128 - value.size))
            for value in (
                jnp.concatenate([attention_total, forward_total, squares[:7]]),
                vector_squares,
                squares[7:],
            )
        ]
    )
    rest = jnp.concatenate(
        [attention_sums, attention_ratios]
        + [
            part[:, piece * width : (piece + 1) * width]
            for part in (forward_sums, forward_ratios)
            for piece in range(pieces)
        ]
        + [jnp.pad(line, (0, width - line.size))[None], small],
        0,
    )
    def over_bands(copies):
        return exchange(copies) if rings == 1 else lax.psum(copies, SEQ)

    copies = bands if rings == 1 else 1
    rest = tie(jnp.broadcast_to(rest, (copies, *rest.shape)), second_piece)
    rest_sums = over_bands(rest)
    patch_own_sum = sum_pairs(tie(jnp.concatenate([first_piece, second_piece], 1), rest))
    patch_gradient, patch_rows_new, pack = patch_statistics(
        patch_own_sum, other_core(patch_own_sum), patch_rows, copies
    )
    pack = over_bands(tie(pack, rest_sums))
    (
        attention_weight_new,
        attention_columns_new,
        forward_weight_new,
        forward_columns_new,
        vectors_new,
        lead_new,
        patch_square,
    ) = finish_rest(
        rest_sums,
        (attention_gradient, attention_weight, attention_rows_new, attention_columns),
        (forward_gradient, forward_weight, forward_rows_new, forward_columns),
        vectors,
        vector_update,
        lead_average,
        band_count,
    )
    patch_rows_line = patch_rows_new[:, 0]
    pack, patch_rows_line = lax.optimization_barrier((pack, patch_rows_line))
    patch_weight_new, patch_columns_new = finish_patch(
        pack, patch_square, patch_gradient, patch_weight, patch_rows_new, patch_columns, band_count
    )
    lead_stats = lead_new[:, : lead_average.size].reshape(2, *lead_average.shape)
    return (
        residual_two.astype(low),
        expert_gates,
        pixel_gradient,
        patch_gradient,
        attention_gradient,
        forward_gradient,
        vector_gradient,
        patch_rows_line,
        patch_columns_new[0],
        attention_rows_new,
        attention_columns_new,
        forward_rows_new,
        forward_columns_new,
        vector_second_new,
        patch_weight_new,
        attention_weight_new,
        forward_weight_new,
        vectors_new,
        lead_stats,
    )


def solution(mesh):
    seq, dp = mesh.shape["seq"], mesh.shape["dp"]
    cores = 2 if dp % 2 == 0 else 1
    dp_axes = ("pair", "core")
    row_spec = P(None, SEQ, None)

    def step(*arguments):
        bands = math.gcd(arguments[0].shape[0] // dp * H, seq)
        grid_mesh = Mesh(
            mesh.devices.reshape(seq // bands, bands, dp // cores, cores),
            ("ring", "band", "pair", "core"),
        )
        return jax.shard_map(
            local,
            mesh=grid_mesh,
            in_specs=(
                P(dp_axes, SEQ, None),
                P(dp_axes, None),
                P(dp_axes),
                P(SEQ, None),
                row_spec,
                row_spec,
                P(None, SEQ),
                P(SEQ),
                P(),
                P(None, SEQ),
                P(),
                P(None, SEQ),
                P(),
                P(None, SEQ),
                P(),
                P(dp_axes, SEQ, None),
                P(dp_axes, None, SEQ),
            ),
            out_specs=(
                P(dp_axes, SEQ, None),
                P(dp_axes, None, SEQ),
                P(dp_axes, SEQ, None),
                P(SEQ, None),
                row_spec,
                row_spec,
                P(None, SEQ),
                P(SEQ),
                P(),
                P(None, SEQ),
                P(),
                P(None, SEQ),
                P(),
                P(None, SEQ),
                P(SEQ, None),
                row_spec,
                row_spec,
                P(None, SEQ),
                P(),
            ),
            check_vma=False,
        )(*arguments)

    return step
```
